32 devices in a mesh: group: 2 (over x), row: 16 (over z, y, core).
Axes of the slice: x: 2, y: 2, z: 4, core: 2. Of those that a mesh axis runs over, the one named last changes fastest.
Arguments:
- orbitals: bfloat16 [8192, 2048], P(('group', 'row')), parts along dimension 0, may hold values from -6 to 6
- rotation: bfloat16 [8192, 2048], P(('group', 'row')), parts along dimension 0, may hold values from -6 to 6
- fock_tiles: bfloat16 [64, 5, 128, 128], P(('group', 'row')), parts along dimension 0, may hold values from -1 to 1, as said below
- fock_pattern: int32 [64, 5], P(('group', 'row')), parts along dimension 0, may hold values from 0 to 1, as said below
- correlation_tiles: bfloat16 [64, 5, 128, 128], P(('group', 'row')), parts along dimension 0, may hold values from -1 to 2, as said below
- correlation_pattern: int32 [64, 5], P(('group', 'row')), parts along dimension 0, may hold values from 0 to 1, as said below
Outputs:
- rotated: bfloat16 [8192, 2048], P(('group', 'row')), parts along dimension 0
- fock_rotated: float32 [8192, 2048], P(('group', 'row')), parts along dimension 0
The draws below stay inside these ranges and needn't reach their ends.
There are 2 independent parts, one for each index of `group`. The reference program is written for one: setup_inputs(seed, part) draws one part's arguments, and reference() takes and returns one part's arrays. A program takes and returns all parts, laid end to end along the dimension named above; each array names one. Nothing has to cross between parts.
Inputs may be any that keep to these rules, and one draw needn't show every extreme that they name: `correlation_tiles`: symmetric: slot j of block row b is the transpose of slot 4 - j of block row b + j - 2 where both lie inside the matrix. `fock_tiles`: symmetric: slot j of block row b is the transpose of slot 4 - j of block row b + j - 2 where both lie inside the matrix. `fock_pattern`: slot j of block row b equals slot 4 - j of block row b + j - 2 where both lie inside the matrix. `correlation_pattern`: slot j of block row b equals slot 4 - j of block row b + j - 2 where both lie inside the matrix.
All inputs are finite; a program needn't handle non-finite values.
Results may differ from the reference program's by a relative error of at most 0.012.
The reference program's roundings to bfloat16 on the way count: a program that leaves them out, or rounds other values in their place, can miss the bound.
Values may be sent and summed in bfloat16 or wider, within the bound.
A program may use at most 128 MiB of HBM per device.

```python
import math
import jax
import jax.numpy as jnp
from jax import lax

TB = 128
M = 2048
ORDER = 5
NB = 32
NBASIS = 4096


def symmetric_band(base_tiles):
    middle = (base_tiles[:, 2] + jnp.swapaxes(base_tiles[:, 2], -1, -2)) * math.sqrt(0.5)
    lower_one = jnp.swapaxes(jnp.roll(base_tiles[:, 3], 1, axis=0), -1, -2)
    lower_two = jnp.swapaxes(jnp.roll(base_tiles[:, 4], 2, axis=0), -1, -2)
    return jnp.stack([lower_two, lower_one, middle, base_tiles[:, 3], base_tiles[:, 4]], axis=1)


def symmetric_pattern(key):
    upper = (jax.random.randint(key, (NB, 5), 0, 3) > 0).astype(jnp.int32)
    lower_one = jnp.roll(upper[:, 3], 1, axis=0)
    lower_two = jnp.roll(upper[:, 4], 2, axis=0)
    return jnp.stack([lower_two, lower_one, upper[:, 2], upper[:, 3], upper[:, 4]], axis=1)


def draw_fock_pattern(key, part):
    key = jax.random.fold_in(key, 21)
    return symmetric_pattern(key)


def draw_correlation_pattern(key, part):
    key = jax.random.fold_in(key, 23)
    return symmetric_pattern(key)


def draw_fock_tiles(key, part):
    key = jax.random.fold_in(key, 13)
    base_tiles = jax.random.truncated_normal(key, -4.0, 4.0, (NB, 5, TB, TB), jnp.float32)
    base_tiles = base_tiles * (1.0 / math.sqrt(5.0 * TB))
    return symmetric_band(base_tiles).astype(jnp.bfloat16)


def draw_correlation_tiles(key, part):
    key = jax.random.fold_in(key, 11)
    off_key, diag_key = jax.random.split(key)
    rough_part = jax.random.truncated_normal(off_key, -4.0, 4.0, (NB, 5, TB, TB), jnp.float32)
    rough_part = symmetric_band(rough_part * (0.5 / math.sqrt(5.0 * TB)))
    diag_values = jax.random.uniform(diag_key, (NB, 1, TB, 1), jnp.float32, 0.6, 1.4)
    shape_full = (NB, 5, TB, TB)
    on_diagonal = (lax.broadcasted_iota(jnp.int32, shape_full, 2) == lax.broadcasted_iota(jnp.int32, shape_full, 3)) & (lax.broadcasted_iota(jnp.int32, shape_full, 1) == 2)
    return (rough_part + jnp.where(on_diagonal, diag_values, 0.0)).astype(jnp.bfloat16)


def levels(key, shape, pieces, low, high):
    def one(position, blocks):
        steps = jax.random.uniform(jax.random.fold_in(jax.random.fold_in(key, 6), position), (blocks,), jnp.float32, low / len(pieces), high / len(pieces))
        return jnp.repeat(jnp.exp(steps), shape[position] // blocks).reshape((-1,) + (1,) * (len(shape) - position - 1))

    gain = one(*pieces[0])
    for cut in pieces[1:]:
        gain = gain * one(*cut)
    return gain


def scatter_about(key, shape, scale, bound, pieces=(), held_as=jnp.bfloat16):
    factor_of = levels(key, shape, pieces, -0.22, 0.18) if pieces else 1.0
    values = jax.random.normal(key, shape, jnp.float32) * scale * factor_of
    return jnp.minimum(jnp.maximum(values, -bound), bound).astype(held_as)


def setup_inputs(seed: int = 0, part: int = 0) -> dict:
    streams_of = jax.random.split(jax.random.key(seed), 7)
    part_keys = jax.random.split(jax.random.fold_in(streams_of[6], part), 7)
    return {
        "orbitals": scatter_about(part_keys[0], (NBASIS, M), 1.0, 6.0, ((0, 16),)),
        "rotation": scatter_about(part_keys[1], (NBASIS, M), 1.0, 6.0, ((0, 16),)),
        "fock_tiles": draw_fock_tiles(jax.random.fold_in(jax.random.fold_in(streams_of[6], part), 71), part),
        "fock_pattern": draw_fock_pattern(jax.random.fold_in(jax.random.fold_in(streams_of[6], part), 71), part),
        "correlation_tiles": draw_correlation_tiles(jax.random.fold_in(jax.random.fold_in(streams_of[6], part), 71), part),
        "correlation_pattern": draw_correlation_pattern(jax.random.fold_in(jax.random.fold_in(streams_of[6], part), 71), part),
    }


def apply_tiles(tile_values, pattern, field_rows):
    block_count = tile_values.shape[0]
    tile_size = tile_values.shape[2]
    slot_ids = lax.broadcasted_iota(jnp.int32, pattern.shape, 1)
    live_mask = (pattern > 0) | (slot_ids == 2)
    padded = jnp.pad(field_rows.astype(jnp.float32), ((2 * tile_size, 2 * tile_size), (0, 0)))
    blocks = padded.reshape(block_count + 4, tile_size, field_rows.shape[1])
    accumulated = jnp.zeros((block_count, tile_size, field_rows.shape[1]), jnp.float32)
    for slot_index in range(5):
        masked_tile = jnp.where(live_mask[:, slot_index, None, None], tile_values[:, slot_index].astype(jnp.float32), jnp.zeros((), jnp.float32))
        accumulated = accumulated + jnp.einsum("bij,bjm->bim", masked_tile, blocks[slot_index:slot_index + block_count])
    return accumulated.reshape(block_count * tile_size, field_rows.shape[1])


def reference(orbitals, rotation, fock_tiles, fock_pattern, correlation_tiles, correlation_pattern):
    cos_coeffs = [(-1.0) ** degree / math.factorial(2 * degree) for degree in range(ORDER + 1)]
    sin_coeffs = [(-1.0) ** degree / math.factorial(2 * degree + 1) for degree in range(ORDER + 1)]
    correlation_applied = apply_tiles(correlation_tiles, correlation_pattern, rotation).astype(jnp.bfloat16)
    gram = jnp.dot(rotation.astype(jnp.float32).T, correlation_applied.astype(jnp.float32), preferred_element_type=jnp.float32)
    gram_low = (gram * (4.0 / NBASIS)).astype(jnp.bfloat16)
    orbitals_wide = orbitals.astype(jnp.float32)
    rotation_wide = rotation.astype(jnp.float32)
    current = (cos_coeffs[ORDER] * orbitals_wide + sin_coeffs[ORDER] * rotation_wide).astype(jnp.bfloat16)
    for degree in range(ORDER - 1, -1, -1):
        summed = jnp.dot(current.astype(jnp.float32), gram_low.astype(jnp.float32), preferred_element_type=jnp.float32)
        current = (summed + cos_coeffs[degree] * orbitals_wide + sin_coeffs[degree] * rotation_wide).astype(jnp.bfloat16)
    rotated = current
    fock_rotated = apply_tiles(fock_tiles, fock_pattern, rotated)
    return rotated, fock_rotated
```

```python
import functools
import math

import jax
import jax.numpy as jnp
from jax import lax
from jax.experimental import pallas as pl
from jax.experimental.pallas import tpu as pltpu
from jax.sharding import PartitionSpec as P

ORDER = 5
BLOCK = 128
SENT = jnp.bfloat16


def halo(value, width):
    size, length = lax.axis_size("row"), value.shape[0]
    up = [(i, i + 1) for i in range(size - 1)]
    down = [(j, i) for i, j in up]
    before = lax.ppermute(value[length - width :], "row", up)
    after = lax.ppermute(value[:width], "row", down)
    return jnp.concatenate([before, value, after], axis=0)


def near_product(tile_values, pattern, extended, blocks_dev, tile_size):
    orbital_count = extended.shape[1]
    blocks = extended.reshape(blocks_dev + 4, tile_size, orbital_count)
    slot_ids = lax.broadcasted_iota(jnp.int32, pattern.shape, 1)
    live_mask = (pattern > 0) | (slot_ids == 2)
    masked = jnp.where(live_mask[:, :, None, None], tile_values, jnp.zeros((), jnp.bfloat16))
    outs = []
    for b in range(blocks_dev):
        wide = jnp.swapaxes(masked[b], 0, 1).reshape(tile_size, 5 * tile_size)
        field = blocks[b : b + 5].reshape(5 * tile_size, orbital_count)
        outs.append(jnp.dot(wide, field, preferred_element_type=jnp.float32))
    return jnp.concatenate(outs, axis=0)


def gram_kernel(half, rot_ref, app_ref, out_ref):
    blocks = rot_ref.shape[1] // BLOCK
    width = (half + 1) * BLOCK
    for i in range(blocks):
        left = rot_ref[:, i * BLOCK : (i + 1) * BLOCK]
        start = i * BLOCK
        first = min(width, rot_ref.shape[1] - start)
        spans = [(0, start, first)]
        if first < width:
            spans.append((first, 0, width - first))
        for at, col, wide in spans:
            out_ref[i * BLOCK : (i + 1) * BLOCK, at : at + wide] = lax.dot_general(
                left,
                app_ref[:, col : col + wide],
                (((0,), (0,)), ((), ())),
                preferred_element_type=jnp.float32,
            ).astype(out_ref.dtype)


def horner_kernel(half, coeffs, packed_ref, orb_ref, rot_ref, out_ref, full):
    blocks = orb_ref.shape[1] // BLOCK
    cos_coeffs, sin_coeffs = coeffs
    for i in range(blocks):
        for k in range(half + 1):
            j = (i + k) % blocks
            tile = packed_ref[i * BLOCK : (i + 1) * BLOCK, k * BLOCK : (k + 1) * BLOCK]
            full[i * BLOCK : (i + 1) * BLOCK, j * BLOCK : (j + 1) * BLOCK] = tile
            if 0 < k < half:
                full[j * BLOCK : (j + 1) * BLOCK, i * BLOCK : (i + 1) * BLOCK] = tile.T
    orb = orb_ref[...].astype(jnp.float32)
    rot = rot_ref[...].astype(jnp.float32)
    current = (cos_coeffs[ORDER] * orb + sin_coeffs[ORDER] * rot).astype(jnp.bfloat16)
    columns = 512
    for degree in range(ORDER - 1, -1, -1):
        parts = []
        for c in range(0, orb_ref.shape[1], columns):
            total = jnp.dot(current, full[:, c : c + columns], preferred_element_type=jnp.float32)
            o = orb_ref[:, c : c + columns].astype(jnp.float32)
            r = rot_ref[:, c : c + columns].astype(jnp.float32)
            parts.append(
                (total + cos_coeffs[degree] * o + sin_coeffs[degree] * r).astype(jnp.bfloat16)
            )
        current = jnp.concatenate(parts, axis=1)
    out_ref[...] = current


def partners(size, bit):
    return [(i, i ^ bit) for i in range(size)]


def reduce_half(value, bit, sent):
    size = lax.axis_size("row")
    high = (lax.axis_index("row") & bit) != 0
    rows = value.shape[0] // 2
    low_part, high_part = value[:rows], value[rows:]
    send = jnp.where(high, low_part, high_part).astype(sent)
    keep = jnp.where(high, high_part, low_part)
    got = lax.ppermute(send, "row", partners(size, bit))
    return keep.astype(jnp.float32) + got.astype(jnp.float32)


def gather_half(value, bit):
    size = lax.axis_size("row")
    high = (lax.axis_index("row") & bit) != 0
    got = lax.ppermute(value, "row", partners(size, bit))
    return jnp.concatenate([jnp.where(high, got, value), jnp.where(high, value, got)], axis=0)


def shards(orbitals, rotation, fock_tiles, fock_pattern, correlation_tiles, correlation_pattern):
    blocks_dev = correlation_tiles.shape[0]
    tile_size = correlation_tiles.shape[2]
    local_rows, orbital_count = rotation.shape
    size = lax.axis_size("row")
    basis_total = local_rows * size
    half = orbital_count // BLOCK // 2
    width = (half + 1) * BLOCK
    cos_coeffs = [(-1.0) ** degree / math.factorial(2 * degree) for degree in range(ORDER + 1)]
    sin_coeffs = [(-1.0) ** degree / math.factorial(2 * degree + 1) for degree in range(ORDER + 1)]
    extended = halo(rotation, 2 * tile_size)
    applied = near_product(
        correlation_tiles, correlation_pattern, extended, blocks_dev, tile_size
    ).astype(jnp.bfloat16)
    packed = pl.pallas_call(
        functools.partial(gram_kernel, half),
        out_shape=jax.ShapeDtypeStruct((orbital_count, width), FIRST),
        in_specs=[pl.BlockSpec(memory_space=pltpu.VMEM)] * 2,
        out_specs=pl.BlockSpec(memory_space=pltpu.VMEM),
        compiler_params=pltpu.CompilerParams(vmem_limit_bytes=40 * 2**20),
    )(rotation, applied)

    share = reduce_half(packed, 1, FIRST)
    bits = [1 << b for b in range(1, size.bit_length() - 1)]
    other = [bits[1], bits[0]] + bits[2:] if len(bits) > 1 else bits
    rows = share.shape[0] // 2
    tracks = [(share[:rows], bits), (share[rows:], other)]
    values = [value for value, _ in tracks]
    for step in range(len(bits)):
        values = [
            reduce_half(value, order[step], SENT) for value, (_, order) in zip(values, tracks)
        ]
    values = [(value * (4.0 / basis_total)).astype(jnp.bfloat16) for value in values]
    for step in range(len(bits) - 1, -1, -1):
        values = [gather_half(value, order[step]) for value, (_, order) in zip(values, tracks)]
    gram_low = gather_half(jnp.concatenate(values, axis=0), 1)

    rotated = pl.pallas_call(
        functools.partial(horner_kernel, half, (cos_coeffs, sin_coeffs)),
        out_shape=jax.ShapeDtypeStruct((local_rows, orbital_count), jnp.bfloat16),
        in_specs=[pl.BlockSpec(memory_space=pltpu.VMEM)] * 3,
        out_specs=pl.BlockSpec(memory_space=pltpu.VMEM),
        scratch_shapes=[pltpu.VMEM((orbital_count, orbital_count), jnp.bfloat16)],
        compiler_params=pltpu.CompilerParams(vmem_limit_bytes=48 * 2**20),
    )(gram_low, orbitals, rotation)
    rotated_ext = halo(rotated, 2 * tile_size)
    fock_rotated = near_product(fock_tiles, fock_pattern, rotated_ext, blocks_dev, tile_size)
    return (rotated, fock_rotated)


FIRST = jnp.bfloat16


def solution(mesh):
    rows = P(("group", "row"), None)
    tiles = P(("group", "row"), None, None, None)
    return jax.shard_map(
        shards,
        mesh=mesh,
        in_specs=(rows, rows, tiles, rows, tiles, rows),
        out_specs=(rows, rows),
        check_vma=False,
    )
```

```python
import functools
import math

import jax
import jax.numpy as jnp
from jax import lax
from jax.experimental import pallas as pl
from jax.experimental.pallas import tpu as pltpu
from jax.sharding import PartitionSpec as P

ORDER = 5
BLOCK = 128
SENT = jnp.bfloat16
TRACKS = 4


def halo(value, width):
    size, length = lax.axis_size("row"), value.shape[0]
    up = [(i, i + 1) for i in range(size - 1)]
    down = [(j, i) for i, j in up]
    before = lax.ppermute(value[length - width :], "row", up)
    after = lax.ppermute(value[:width], "row", down)
    return jnp.concatenate([before, value, after], axis=0)


def near_product(tile_values, pattern, extended, blocks_dev, tile_size):
    orbital_count = extended.shape[1]
    blocks = extended.reshape(blocks_dev + 4, tile_size, orbital_count)
    slot_ids = lax.broadcasted_iota(jnp.int32, pattern.shape, 1)
    live_mask = (pattern > 0) | (slot_ids == 2)
    masked = jnp.where(live_mask[:, :, None, None], tile_values, jnp.zeros((), jnp.bfloat16))
    outs = []
    for b in range(blocks_dev):
        wide = jnp.swapaxes(masked[b], 0, 1).reshape(tile_size, 5 * tile_size)
        field = blocks[b : b + 5].reshape(5 * tile_size, orbital_count)
        outs.append(jnp.dot(wide, field, preferred_element_type=jnp.float32))
    return jnp.concatenate(outs, axis=0)


def gram_kernel(half, rot_ref, app_ref, out_ref):
    blocks = rot_ref.shape[1] // BLOCK
    width = (half + 1) * BLOCK
    for i in range(blocks):
        left = rot_ref[:, i * BLOCK : (i + 1) * BLOCK]
        start = i * BLOCK
        first = min(width, rot_ref.shape[1] - start)
        spans = [(0, start, first)]
        if first < width:
            spans.append((first, 0, width - first))
        for at, col, wide in spans:
            out_ref[i * BLOCK : (i + 1) * BLOCK, at : at + wide] = lax.dot_general(
                left,
                app_ref[:, col : col + wide],
                (((0,), (0,)), ((), ())),
                preferred_element_type=jnp.float32,
            ).astype(out_ref.dtype)


def horner_kernel(half, coeffs, packed_ref, orb_ref, rot_ref, out_ref, full):
    blocks = orb_ref.shape[1] // BLOCK
    cos_coeffs, sin_coeffs = coeffs
    for i in range(blocks):
        for k in range(half + 1):
            j = (i + k) % blocks
            tile = packed_ref[i * BLOCK : (i + 1) * BLOCK, k * BLOCK : (k + 1) * BLOCK]
            full[i * BLOCK : (i + 1) * BLOCK, j * BLOCK : (j + 1) * BLOCK] = tile
            if 0 < k < half:
                full[j * BLOCK : (j + 1) * BLOCK, i * BLOCK : (i + 1) * BLOCK] = tile.T
    orb = orb_ref[...].astype(jnp.float32)
    rot = rot_ref[...].astype(jnp.float32)
    current = (cos_coeffs[ORDER] * orb + sin_coeffs[ORDER] * rot).astype(jnp.bfloat16)
    columns = 512
    for degree in range(ORDER - 1, -1, -1):
        parts = []
        for c in range(0, orb_ref.shape[1], columns):
            total = jnp.dot(current, full[:, c : c + columns], preferred_element_type=jnp.float32)
            o = orb_ref[:, c : c + columns].astype(jnp.float32)
            r = rot_ref[:, c : c + columns].astype(jnp.float32)
            parts.append(
                (total + cos_coeffs[degree] * o + sin_coeffs[degree] * r).astype(jnp.bfloat16)
            )
        current = jnp.concatenate(parts, axis=1)
    out_ref[...] = current


def exchange_kernel(tracks, scale, packed_ref, out_ref, got, acc, send, send_sem, recv_sem):
    size = lax.axis_size("row")
    me = lax.axis_index("row")
    steps = size.bit_length() - 1
    width = packed_ref.shape[1]
    rows = packed_ref.shape[0] // tracks
    half = rows // 2
    outer = [1 << b for b in range(1, steps)]
    swapped = [outer[1], outer[0]] + outer[2:] if len(outer) > 1 else outer
    orders = [[1] + (outer if t % 2 == 0 else swapped) for t in range(tracks)]

    def high(bit):
        return lax.rem(me // bit, 2)

    def partner(bit):
        return me + bit - 2 * bit * high(bit)

    def span(start, count):
        return pl.ds(pl.multiple_of(start, 16), count)

    def copy(source, target, t, step, bit):
        return pltpu.make_async_remote_copy(
            src_ref=source,
            dst_ref=target,
            send_sem=send_sem.at[t, step],
            recv_sem=recv_sem.at[t, step],
            device_id={"row": partner(bit)},
            device_id_type=pl.DeviceIdType.MESH,
        )

    barrier = pltpu.get_barrier_semaphore()
    for b in range(steps):
        pl.semaphore_signal(
            barrier, inc=1, device_id={"row": partner(1 << b)}, device_id_type=pl.DeviceIdType.MESH
        )
    pl.semaphore_wait(barrier, steps)

    copies = []
    pending = []
    offsets = [0] * tracks
    for t in range(tracks):
        c = copy(
            packed_ref.at[span(t * rows + (1 - high(1)) * half, half)],
            got.at[pl.ds(t * rows, half)],
            t, 0, 1,
        )
        c.start()
        copies.append(c)
        pending.append(c)

    for step in range(steps):
        count = rows >> (step + 1)
        landed = rows - (rows >> step)
        for t in range(tracks):
            pending[t].wait_recv()
            base = offsets[t]

            def total(shift, number):
                more = got[span(t * rows + landed + shift, number), :].astype(jnp.float32)
                if step == 0:
                    own = packed_ref[span(t * rows + high(1) * half + shift, number), :]
                    return own.astype(jnp.float32) + more
                return acc[span(t * half + base + shift, number), :] + more

            if step < steps - 1:
                bit = orders[t][step + 1]
                part = count // 2
                away, kept = (1 - high(bit)) * part, high(bit) * part
                place = span(t * half + base + away, part)
                send[place, :] = total(away, part).astype(send.dtype)
                c = copy(
                    send.at[place],
                    got.at[pl.ds(t * rows + landed + count, part)],
                    t, step + 1, bit,
                )
                c.start()
                acc[span(t * half + base + kept, part), :] = total(kept, part)
                offsets[t] = base + kept
            else:
                offsets[t] = t * rows + high(1) * half + base
                place = span(offsets[t], count)
                out_ref[place, :] = (total(0, count) * scale).astype(out_ref.dtype)
                c = copy(out_ref.at[place], out_ref.at[place], t, steps, orders[t][step])
                c.start()
            copies.append(c)
            pending[t] = c

    count = rows >> steps
    for step in range(steps):
        for t in range(tracks):
            bit = orders[t][steps - 1 - step]
            pending[t].wait_recv()
            offsets[t] = offsets[t] - high(bit) * count
            if step < steps - 1:
                place = span(offsets[t], 2 * count)
                c = copy(
                    out_ref.at[place], out_ref.at[place], t, steps + step + 1,
                    orders[t][steps - 2 - step],
                )
                c.start()
                copies.append(c)
                pending[t] = c
        count = 2 * count
    for c in copies:
        c.wait_send()


def exchange(packed, scale):
    size = lax.axis_size("row")
    rows, width = packed.shape
    steps = size.bit_length() - 1
    tracks = max(1, min(TRACKS, rows // (16 * size)))
    return pl.pallas_call(
        functools.partial(exchange_kernel, tracks, scale),
        out_shape=jax.ShapeDtypeStruct((rows, width), jnp.bfloat16),
        in_specs=[pl.BlockSpec(memory_space=pltpu.VMEM)],
        out_specs=pl.BlockSpec(memory_space=pltpu.VMEM),
        scratch_shapes=[
            pltpu.VMEM((rows, width), SENT),
            pltpu.VMEM((rows // 2, width), jnp.float32),
            pltpu.VMEM((rows // 2, width), SENT),
            pltpu.SemaphoreType.DMA((tracks, 2 * steps)),
            pltpu.SemaphoreType.DMA((tracks, 2 * steps)),
        ],
        compiler_params=pltpu.CompilerParams(
            collective_id=0, has_side_effects=True, vmem_limit_bytes=48 * 2**20
        ),
    )(packed)


def shards(orbitals, rotation, fock_tiles, fock_pattern, correlation_tiles, correlation_pattern):
    blocks_dev = correlation_tiles.shape[0]
    tile_size = correlation_tiles.shape[2]
    local_rows, orbital_count = rotation.shape
    size = lax.axis_size("row")
    basis_total = local_rows * size
    half = orbital_count // BLOCK // 2
    width = (half + 1) * BLOCK
    cos_coeffs = [(-1.0) ** degree / math.factorial(2 * degree) for degree in range(ORDER + 1)]
    sin_coeffs = [(-1.0) ** degree / math.factorial(2 * degree + 1) for degree in range(ORDER + 1)]
    extended = halo(rotation, 2 * tile_size)
    applied = near_product(
        correlation_tiles, correlation_pattern, extended, blocks_dev, tile_size
    ).astype(jnp.bfloat16)
    packed = pl.pallas_call(
        functools.partial(gram_kernel, half),
        out_shape=jax.ShapeDtypeStruct((orbital_count, width), SENT),
        in_specs=[pl.BlockSpec(memory_space=pltpu.VMEM)] * 2,
        out_specs=pl.BlockSpec(memory_space=pltpu.VMEM),
        compiler_params=pltpu.CompilerParams(vmem_limit_bytes=40 * 2**20),
    )(rotation, applied)

    gram_low = exchange(packed, 4.0 / basis_total)

    rotated = pl.pallas_call(
        functools.partial(horner_kernel, half, (cos_coeffs, sin_coeffs)),
        out_shape=jax.ShapeDtypeStruct((local_rows, orbital_count), jnp.bfloat16),
        in_specs=[pl.BlockSpec(memory_space=pltpu.VMEM)] * 3,
        out_specs=pl.BlockSpec(memory_space=pltpu.VMEM),
        scratch_shapes=[pltpu.VMEM((orbital_count, orbital_count), jnp.bfloat16)],
        compiler_params=pltpu.CompilerParams(vmem_limit_bytes=48 * 2**20),
    )(gram_low, orbitals, rotation)
    rotated_ext = halo(rotated, 2 * tile_size)
    fock_rotated = near_product(fock_tiles, fock_pattern, rotated_ext, blocks_dev, tile_size)
    return (rotated, fock_rotated)


def solution(mesh):
    rows = P(("group", "row"), None)
    tiles = P(("group", "row"), None, None, None)
    return jax.shard_map(
        shards,
        mesh=mesh,
        in_specs=(rows, rows, tiles, rows, tiles, rows),
        out_specs=(rows, rows),
        check_vma=False,
    )
```

```python
import functools
import math

import jax
import jax.numpy as jnp
from jax import lax
from jax.experimental import pallas as pl
from jax.experimental.pallas import tpu as pltpu
from jax.sharding import PartitionSpec as P

ORDER = 5
BLOCK = 128
SENT = jnp.bfloat16
TRACKS = 8


def halo(value, width):
    size, length = lax.axis_size("row"), value.shape[0]
    up = [(i, i + 1) for i in range(size - 1)]
    down = [(j, i) for i, j in up]
    before = lax.ppermute(value[length - width :], "row", up)
    after = lax.ppermute(value[:width], "row", down)
    return jnp.concatenate([before, value, after], axis=0)


def near_product(tile_values, pattern, extended, blocks_dev, tile_size):
    orbital_count = extended.shape[1]
    blocks = extended.reshape(blocks_dev + 4, tile_size, orbital_count)
    slot_ids = lax.broadcasted_iota(jnp.int32, pattern.shape, 1)
    live_mask = (pattern > 0) | (slot_ids == 2)
    masked = jnp.where(live_mask[:, :, None, None], tile_values, jnp.zeros((), jnp.bfloat16))
    outs = []
    for b in range(blocks_dev):
        wide = jnp.swapaxes(masked[b], 0, 1).reshape(tile_size, 5 * tile_size)
        field = blocks[b : b + 5].reshape(5 * tile_size, orbital_count)
        outs.append(jnp.dot(wide, field, preferred_element_type=jnp.float32))
    return jnp.concatenate(outs, axis=0)


def gram_kernel(half, rot_ref, app_ref, out_ref):
    blocks = rot_ref.shape[1] // BLOCK
    width = (half + 1) * BLOCK
    for i in range(blocks):
        left = rot_ref[:, i * BLOCK : (i + 1) * BLOCK]
        start = i * BLOCK
        first = min(width, rot_ref.shape[1] - start)
        spans = [(0, start, first)]
        if first < width:
            spans.append((first, 0, width - first))
        for at, col, wide in spans:
            out_ref[i * BLOCK : (i + 1) * BLOCK, at : at + wide] = lax.dot_general(
                left,
                app_ref[:, col : col + wide],
                (((0,), (0,)), ((), ())),
                preferred_element_type=jnp.float32,
            ).astype(out_ref.dtype)


def spread(packed_ref, full, first, last):
    blocks = full.shape[0] // BLOCK
    half = packed_ref.shape[1] // BLOCK - 1
    for i in range(first, last):
        for k in range(half + 1):
            j = (i + k) % blocks
            tile = packed_ref[i * BLOCK : (i + 1) * BLOCK, k * BLOCK : (k + 1) * BLOCK]
            full[i * BLOCK : (i + 1) * BLOCK, j * BLOCK : (j + 1) * BLOCK] = tile
            if 0 < k < half:
                full[j * BLOCK : (j + 1) * BLOCK, i * BLOCK : (i + 1) * BLOCK] = tile.T


def horner(coeffs, orb_ref, rot_ref, out_ref, full):
    cos_coeffs, sin_coeffs = coeffs
    orb = orb_ref[...].astype(jnp.float32)
    rot = rot_ref[...].astype(jnp.float32)
    current = (cos_coeffs[ORDER] * orb + sin_coeffs[ORDER] * rot).astype(jnp.bfloat16)
    columns = 512
    for degree in range(ORDER - 1, -1, -1):
        parts = []
        for c in range(0, orb_ref.shape[1], columns):
            total = jnp.dot(current, full[:, c : c + columns], preferred_element_type=jnp.float32)
            o = orb_ref[:, c : c + columns].astype(jnp.float32)
            r = rot_ref[:, c : c + columns].astype(jnp.float32)
            parts.append(
                (total + cos_coeffs[degree] * o + sin_coeffs[degree] * r).astype(jnp.bfloat16)
            )
        current = jnp.concatenate(parts, axis=1)
    out_ref[...] = current


def exchange_kernel(
    tracks, scale, coeffs, packed_ref, orb_ref, rot_ref, rotated_ref,
    got, acc, send, out_ref, full, send_sem, recv_sem,
):
    size = lax.axis_size("row")
    me = lax.axis_index("row")
    steps = size.bit_length() - 1
    width = packed_ref.shape[1]
    rows = packed_ref.shape[0] // tracks
    half = rows // 2
    outer = [1 << b for b in range(1, steps)]
    swapped = [outer[1], outer[0]] + outer[2:] if len(outer) > 1 else outer
    orders = [[1] + (outer if t % 2 == 0 else swapped) for t in range(tracks)]

    def high(bit):
        return lax.rem(me // bit, 2)

    def partner(bit):
        return me + bit - 2 * bit * high(bit)

    def span(start, count):
        return pl.ds(pl.multiple_of(start, 16), count)

    def copy(source, target, t, step, bit):
        return pltpu.make_async_remote_copy(
            src_ref=source,
            dst_ref=target,
            send_sem=send_sem.at[t, step],
            recv_sem=recv_sem.at[t, step],
            device_id={"row": partner(bit)},
            device_id_type=pl.DeviceIdType.MESH,
        )

    barrier = pltpu.get_barrier_semaphore()
    for b in range(steps):
        pl.semaphore_signal(
            barrier, inc=1, device_id={"row": partner(1 << b)}, device_id_type=pl.DeviceIdType.MESH
        )
    pl.semaphore_wait(barrier, steps)

    copies = []
    pending = []
    offsets = [0] * tracks
    for t in range(tracks):
        c = copy(
            packed_ref.at[span(t * rows + (1 - high(1)) * half, half)],
            got.at[pl.ds(t * rows, half)],
            t, 0, 1,
        )
        c.start()
        copies.append(c)
        pending.append(c)

    for step in range(steps):
        count = rows >> (step + 1)
        landed = rows - (rows >> step)
        for t in range(tracks):
            pending[t].wait_recv()
            base = offsets[t]

            def total(shift, number):
                more = got[span(t * rows + landed + shift, number), :].astype(jnp.float32)
                if step == 0:
                    own = packed_ref[span(t * rows + high(1) * half + shift, number), :]
                    return own.astype(jnp.float32) + more
                return acc[span(t * half + base + shift, number), :] + more

            if step < steps - 1:
                bit = orders[t][step + 1]
                part = count // 2
                away, kept = (1 - high(bit)) * part, high(bit) * part
                place = span(t * half + base + away, part)
                send[place, :] = total(away, part).astype(send.dtype)
                c = copy(
                    send.at[place],
                    got.at[pl.ds(t * rows + landed + count, part)],
                    t, step + 1, bit,
                )
                c.start()
                acc[span(t * half + base + kept, part), :] = total(kept, part)
                offsets[t] = base + kept
            else:
                offsets[t] = t * rows + high(1) * half + base
                place = span(offsets[t], count)
                out_ref[place, :] = (total(0, count) * scale).astype(out_ref.dtype)
                c = copy(out_ref.at[place], out_ref.at[place], t, steps, orders[t][step])
                c.start()
            copies.append(c)
            pending[t] = c

    count = rows >> steps
    for step in range(steps):
        for t in range(tracks):
            bit = orders[t][steps - 1 - step]
            pending[t].wait_recv()
            offsets[t] = offsets[t] - high(bit) * count
            if step < steps - 1:
                place = span(offsets[t], 2 * count)
                c = copy(
                    out_ref.at[place], out_ref.at[place], t, steps + step + 1,
                    orders[t][steps - 2 - step],
                )
                c.start()
                copies.append(c)
                pending[t] = c
            else:
                spread(out_ref, full, t * rows // BLOCK, (t + 1) * rows // BLOCK)
        count = 2 * count
    horner(coeffs, orb_ref, rot_ref, rotated_ref, full)
    for c in copies:
        c.wait_send()


def exchange(packed, orbitals, rotation, scale, coeffs):
    size = lax.axis_size("row")
    rows, width = packed.shape
    steps = size.bit_length() - 1
    tracks = max(1, min(TRACKS, rows // (16 * size)))
    return pl.pallas_call(
        functools.partial(exchange_kernel, tracks, scale, coeffs),
        out_shape=jax.ShapeDtypeStruct(orbitals.shape, jnp.bfloat16),
        in_specs=[pl.BlockSpec(memory_space=pltpu.VMEM)] * 3,
        out_specs=pl.BlockSpec(memory_space=pltpu.VMEM),
        scratch_shapes=[
            pltpu.VMEM((rows, width), SENT),
            pltpu.VMEM((rows // 2, width), jnp.float32),
            pltpu.VMEM((rows // 2, width), SENT),
            pltpu.VMEM((rows, width), jnp.bfloat16),
            pltpu.VMEM((rows, rows), jnp.bfloat16),
            pltpu.SemaphoreType.DMA((tracks, 2 * steps)),
            pltpu.SemaphoreType.DMA((tracks, 2 * steps)),
        ],
        compiler_params=pltpu.CompilerParams(
            collective_id=0, has_side_effects=True, vmem_limit_bytes=56 * 2**20
        ),
    )(packed, orbitals, rotation)


def shards(orbitals, rotation, fock_tiles, fock_pattern, correlation_tiles, correlation_pattern):
    blocks_dev = correlation_tiles.shape[0]
    tile_size = correlation_tiles.shape[2]
    local_rows, orbital_count = rotation.shape
    size = lax.axis_size("row")
    basis_total = local_rows * size
    half = orbital_count // BLOCK // 2
    width = (half + 1) * BLOCK
    cos_coeffs = [(-1.0) ** degree / math.factorial(2 * degree) for degree in range(ORDER + 1)]
    sin_coeffs = [(-1.0) ** degree / math.factorial(2 * degree + 1) for degree in range(ORDER + 1)]
    extended = halo(rotation, 2 * tile_size)
    applied = near_product(
        correlation_tiles, correlation_pattern, extended, blocks_dev, tile_size
    ).astype(jnp.bfloat16)
    packed = pl.pallas_call(
        functools.partial(gram_kernel, half),
        out_shape=jax.ShapeDtypeStruct((orbital_count, width), SENT),
        in_specs=[pl.BlockSpec(memory_space=pltpu.VMEM)] * 2,
        out_specs=pl.BlockSpec(memory_space=pltpu.VMEM),
        compiler_params=pltpu.CompilerParams(vmem_limit_bytes=40 * 2**20),
    )(rotation, applied)

    rotated = exchange(
        packed, orbitals, rotation, 4.0 / basis_total, (cos_coeffs, sin_coeffs)
    )
    rotated_ext = halo(rotated, 2 * tile_size)
    fock_rotated = near_product(fock_tiles, fock_pattern, rotated_ext, blocks_dev, tile_size)
    return (rotated, fock_rotated)


def solution(mesh):
    rows = P(("group", "row"), None)
    tiles = P(("group", "row"), None, None, None)
    return jax.shard_map(
        shards,
        mesh=mesh,
        in_specs=(rows, rows, tiles, rows, tiles, rows),
        out_specs=(rows, rows),
        check_vma=False,
    )
```

```python
import functools
import math

import jax
import jax.numpy as jnp
from jax import lax
from jax.experimental import pallas as pl
from jax.experimental.pallas import tpu as pltpu
from jax.sharding import PartitionSpec as P

ORDER = 5
BLOCK = 128
SENT = jnp.bfloat16
TRACKS = 8
CHUNK = 512


def halo(value, width):
    size, length = lax.axis_size("row"), value.shape[0]
    up = [(i, i + 1) for i in range(size - 1)]
    down = [(j, i) for i, j in up]
    before = lax.ppermute(value[length - width :], "row", up)
    after = lax.ppermute(value[:width], "row", down)
    return jnp.concatenate([before, value, after], axis=0)


def wide_tiles(tile_values, pattern):
    blocks_dev, slots, tile_size, _ = tile_values.shape
    slot_ids = lax.broadcasted_iota(jnp.int32, pattern.shape, 1)
    live_mask = (pattern > 0) | (slot_ids == 2)
    masked = jnp.where(live_mask[:, :, None, None], tile_values, jnp.zeros((), jnp.bfloat16))
    return jnp.swapaxes(masked, 1, 2).reshape(blocks_dev * tile_size, slots * tile_size)


def near_product(wide, extended):
    return jnp.concatenate(
        [
            jnp.dot(
                wide[at : at + BLOCK],
                extended[at : at + 5 * BLOCK],
                preferred_element_type=jnp.float32,
            )
            for at in range(0, wide.shape[0], BLOCK)
        ],
        axis=0,
    )


def gram_kernel(half, rot_ref, app_ref, out_ref):
    blocks = rot_ref.shape[1] // BLOCK
    width = (half + 1) * BLOCK
    for i in range(blocks):
        left = rot_ref[:, i * BLOCK : (i + 1) * BLOCK]
        start = i * BLOCK
        first = min(width, rot_ref.shape[1] - start)
        spans = [(0, start, first)]
        if first < width:
            spans.append((first, 0, width - first))
        for at, col, wide in spans:
            out_ref[i * BLOCK : (i + 1) * BLOCK, at : at + wide] = lax.dot_general(
                left,
                app_ref[:, col : col + wide],
                (((0,), (0,)), ((), ())),
                preferred_element_type=jnp.float32,
            ).astype(out_ref.dtype)


def spread(packed_ref, full, first, last):
    blocks = full.shape[0] // BLOCK
    half = packed_ref.shape[1] // BLOCK - 1
    for i in range(first, last):
        for k in range(half + 1):
            j = (i + k) % blocks
            tile = packed_ref[i * BLOCK : (i + 1) * BLOCK, k * BLOCK : (k + 1) * BLOCK]
            full[i * BLOCK : (i + 1) * BLOCK, j * BLOCK : (j + 1) * BLOCK] = tile
            if 0 < k < half:
                full[j * BLOCK : (j + 1) * BLOCK, i * BLOCK : (i + 1) * BLOCK] = tile.T


def horner(coeffs, orb_ref, rot_ref, full, columns, emit):
    cos_coeffs, sin_coeffs = coeffs
    orb = orb_ref[...].astype(jnp.float32)
    rot = rot_ref[...].astype(jnp.float32)
    current = (cos_coeffs[ORDER] * orb + sin_coeffs[ORDER] * rot).astype(jnp.bfloat16)
    for degree in range(ORDER - 1, -1, -1):
        parts = []
        for c in range(0, orb_ref.shape[1], columns):
            total = jnp.dot(current, full[:, c : c + columns], preferred_element_type=jnp.float32)
            o = orb_ref[:, c : c + columns].astype(jnp.float32)
            r = rot_ref[:, c : c + columns].astype(jnp.float32)
            part = (total + cos_coeffs[degree] * o + sin_coeffs[degree] * r).astype(jnp.bfloat16)
            if degree == 0:
                emit(c, part)
            parts.append(part)
        if degree:
            current = jnp.concatenate(parts, axis=1)


def exchange_kernel(
    tracks, scale, coeffs, packed_ref, orb_ref, rot_ref, wide_ref, rotated_ref, fock_ref,
    got, acc, send, out_ref, full, ext, send_sem, recv_sem, halo_send, halo_recv,
):
    size = lax.axis_size("row")
    me = lax.axis_index("row")
    steps = size.bit_length() - 1
    width = packed_ref.shape[1]
    rows = packed_ref.shape[0] // tracks
    half = rows // 2
    outer = [1 << b for b in range(1, steps)]
    swapped = [outer[1], outer[0]] + outer[2:] if len(outer) > 1 else outer
    orders = [[1] + (outer if t % 2 == 0 else swapped) for t in range(tracks)]

    def high(bit):
        return lax.rem(me // bit, 2)

    def partner(bit):
        return me + bit - 2 * bit * high(bit)

    def span(start, count):
        return pl.ds(pl.multiple_of(start, 16), count)

    def copy(source, target, t, step, bit):
        return pltpu.make_async_remote_copy(
            src_ref=source,
            dst_ref=target,
            send_sem=send_sem.at[t, step],
            recv_sem=recv_sem.at[t, step],
            device_id={"row": partner(bit)},
            device_id_type=pl.DeviceIdType.MESH,
        )

    barrier = pltpu.get_barrier_semaphore()
    for b in range(steps):
        pl.semaphore_signal(
            barrier, inc=1, device_id={"row": partner(1 << b)}, device_id_type=pl.DeviceIdType.MESH
        )
    below, above = me > 0, me < size - 1
    inner = jnp.logical_and(below, above)

    @pl.when(inner)
    def _():
        pl.semaphore_signal(
            barrier,
            inc=1,
            device_id={"row": me - 1 + 2 * lax.rem(me, 2)},
            device_id_type=pl.DeviceIdType.MESH,
        )
        pl.semaphore_wait(barrier, steps + 1)

    @pl.when(jnp.logical_not(inner))
    def _():
        pl.semaphore_wait(barrier, steps)

    local, wing = orb_ref.shape[0], 2 * BLOCK

    @pl.when(me == 0)
    def _():
        ext[:wing, :] = jnp.zeros((wing, ext.shape[1]), ext.dtype)

    @pl.when(me == size - 1)
    def _():
        ext[local + wing :, :] = jnp.zeros((wing, ext.shape[1]), ext.dtype)

    copies = []
    pending = []
    offsets = [0] * tracks
    for t in range(tracks):
        c = copy(
            packed_ref.at[span(t * rows + (1 - high(1)) * half, half)],
            got.at[pl.ds(t * rows, half)],
            t, 0, 1,
        )
        c.start()
        copies.append(c)
        pending.append(c)

    for step in range(steps):
        count = rows >> (step + 1)
        landed = rows - (rows >> step)
        for t in range(tracks):
            pending[t].wait_recv()
            base = offsets[t]

            def total(shift, number):
                more = got[span(t * rows + landed + shift, number), :].astype(jnp.float32)
                if step == 0:
                    own = packed_ref[span(t * rows + high(1) * half + shift, number), :]
                    return own.astype(jnp.float32) + more
                return acc[span(t * half + base + shift, number), :] + more

            if step < steps - 1:
                bit = orders[t][step + 1]
                part = count // 2
                away, kept = (1 - high(bit)) * part, high(bit) * part
                place = span(t * half + base + away, part)
                send[place, :] = total(away, part).astype(send.dtype)
                c = copy(
                    send.at[place],
                    got.at[pl.ds(t * rows + landed + count, part)],
                    t, step + 1, bit,
                )
                c.start()
                acc[span(t * half + base + kept, part), :] = total(kept, part)
                offsets[t] = base + kept
            else:
                offsets[t] = t * rows + high(1) * half + base
                place = span(offsets[t], count)
                out_ref[place, :] = (total(0, count) * scale).astype(out_ref.dtype)
                c = copy(out_ref.at[place], out_ref.at[place], t, steps, orders[t][step])
                c.start()
            copies.append(c)
            pending[t] = c

    count = rows >> steps
    for step in range(steps):
        for t in range(tracks):
            bit = orders[t][steps - 1 - step]
            pending[t].wait_recv()
            offsets[t] = offsets[t] - high(bit) * count
            if step < steps - 1:
                place = span(offsets[t], 2 * count)
                c = copy(
                    out_ref.at[place], out_ref.at[place], t, steps + step + 1,
                    orders[t][steps - 2 - step],
                )
                c.start()
                copies.append(c)
                pending[t] = c
            else:
                spread(out_ref, full, t * rows // BLOCK, (t + 1) * rows // BLOCK)
        count = 2 * count

    columns = CHUNK

    def halo_copy(side, c):
        source, target, index = ((wing, local + wing, me - 1), (local, 0, me + 1))[side]
        return pltpu.make_async_remote_copy(
            src_ref=ext.at[pl.ds(source, wing), pl.ds(c, columns)],
            dst_ref=ext.at[pl.ds(target, wing), pl.ds(c, columns)],
            send_sem=halo_send.at[side, c // columns],
            recv_sem=halo_recv.at[side, c // columns],
            device_id={"row": index},
            device_id_type=pl.DeviceIdType.MESH,
        )

    def emit(c, part):
        rotated_ref[:, c : c + columns] = part
        ext[wing : wing + local, c : c + columns] = part
        for side, there in ((0, below), (1, above)):

            @pl.when(there)
            def _():
                halo_copy(side, c).start()

    horner(coeffs, orb_ref, rot_ref, full, columns, emit)
    for c in range(0, orb_ref.shape[1], columns):
        for side, there in ((0, above), (1, below)):

            @pl.when(there)
            def _():
                halo_copy(side, c).wait_recv()

        for at in range(0, local, BLOCK):
            fock_ref[at : at + BLOCK, c : c + columns] = jnp.dot(
                wide_ref[at : at + BLOCK, :],
                ext[at : at + 5 * BLOCK, c : c + columns],
                preferred_element_type=jnp.float32,
            )
    for c in range(0, orb_ref.shape[1], columns):
        for side, there in ((0, below), (1, above)):

            @pl.when(there)
            def _():
                halo_copy(side, c).wait_send()

    for c in copies:
        c.wait_send()


def exchange(packed, orbitals, rotation, wide, scale, coeffs):
    size = lax.axis_size("row")
    rows, width = packed.shape
    steps = size.bit_length() - 1
    tracks = max(1, min(TRACKS, rows // (16 * size)))
    return pl.pallas_call(
        functools.partial(exchange_kernel, tracks, scale, coeffs),
        out_shape=(
            jax.ShapeDtypeStruct(orbitals.shape, jnp.bfloat16),
            jax.ShapeDtypeStruct(orbitals.shape, jnp.float32),
        ),
        in_specs=[pl.BlockSpec(memory_space=pltpu.VMEM)] * 4,
        out_specs=(pl.BlockSpec(memory_space=pltpu.VMEM),) * 2,
        scratch_shapes=[
            pltpu.VMEM((rows, width), SENT),
            pltpu.VMEM((rows // 2, width), jnp.float32),
            pltpu.VMEM((rows // 2, width), SENT),
            pltpu.VMEM((rows, width), jnp.bfloat16),
            pltpu.VMEM((rows, rows), jnp.bfloat16),
            pltpu.VMEM((orbitals.shape[0] + 4 * BLOCK, rows), jnp.bfloat16),
            pltpu.SemaphoreType.DMA((tracks, 2 * steps)),
            pltpu.SemaphoreType.DMA((tracks, 2 * steps)),
            pltpu.SemaphoreType.DMA((2, rows // CHUNK)),
            pltpu.SemaphoreType.DMA((2, rows // CHUNK)),
        ],
        compiler_params=pltpu.CompilerParams(
            collective_id=0, has_side_effects=True, vmem_limit_bytes=56 * 2**20
        ),
    )(packed, orbitals, rotation, wide)


def shards(orbitals, rotation, fock_tiles, fock_pattern, correlation_tiles, correlation_pattern):
    tile_size = correlation_tiles.shape[2]
    local_rows, orbital_count = rotation.shape
    size = lax.axis_size("row")
    basis_total = local_rows * size
    half = orbital_count // BLOCK // 2
    width = (half + 1) * BLOCK
    cos_coeffs = [(-1.0) ** degree / math.factorial(2 * degree) for degree in range(ORDER + 1)]
    sin_coeffs = [(-1.0) ** degree / math.factorial(2 * degree + 1) for degree in range(ORDER + 1)]
    extended = halo(rotation, 2 * tile_size)
    applied = near_product(wide_tiles(correlation_tiles, correlation_pattern), extended)
    applied = applied.astype(jnp.bfloat16)
    packed = pl.pallas_call(
        functools.partial(gram_kernel, half),
        out_shape=jax.ShapeDtypeStruct((orbital_count, width), SENT),
        in_specs=[pl.BlockSpec(memory_space=pltpu.VMEM)] * 2,
        out_specs=pl.BlockSpec(memory_space=pltpu.VMEM),
        compiler_params=pltpu.CompilerParams(vmem_limit_bytes=40 * 2**20),
    )(rotation, applied)

    wide = wide_tiles(fock_tiles, fock_pattern)
    return exchange(
        packed, orbitals, rotation, wide, 4.0 / basis_total, (cos_coeffs, sin_coeffs)
    )


def solution(mesh):
    rows = P(("group", "row"), None)
    tiles = P(("group", "row"), None, None, None)
    return jax.shard_map(
        shards,
        mesh=mesh,
        in_specs=(rows, rows, tiles, rows, tiles, rows),
        out_specs=(rows, rows),
        check_vma=False,
    )
```

```python
import functools
import math

import jax
import jax.numpy as jnp
from jax import lax
from jax.experimental import pallas as pl
from jax.experimental.pallas import tpu as pltpu
from jax.sharding import PartitionSpec as P

ORDER = 5
BLOCK = 128
SENT = jnp.bfloat16
TRACKS = 8
CHUNK = 512


def halo(value, width):
    size, length = lax.axis_size("row"), value.shape[0]
    up = [(i, i + 1) for i in range(size - 1)]
    down = [(j, i) for i, j in up]
    before = lax.ppermute(value[length - width :], "row", up)
    after = lax.ppermute(value[:width], "row", down)
    return jnp.concatenate([before, value, after], axis=0)


def wide_tiles(tile_values, pattern):
    blocks_dev, slots, tile_size, _ = tile_values.shape
    slot_ids = lax.broadcasted_iota(jnp.int32, pattern.shape, 1)
    live_mask = (pattern > 0) | (slot_ids == 2)
    masked = jnp.where(live_mask[:, :, None, None], tile_values, jnp.zeros((), jnp.bfloat16))
    return jnp.swapaxes(masked, 1, 2).reshape(blocks_dev * tile_size, slots * tile_size)


def near_product(wide, extended):
    return jnp.concatenate(
        [
            jnp.dot(
                wide[at : at + BLOCK],
                extended[at : at + 5 * BLOCK],
                preferred_element_type=jnp.float32,
            )
            for at in range(0, wide.shape[0], BLOCK)
        ],
        axis=0,
    )


def gram_kernel(half, rot_ref, app_ref, out_ref):
    blocks = rot_ref.shape[1] // BLOCK
    width = (half + 1) * BLOCK
    for i in range(blocks):
        left = rot_ref[:, i * BLOCK : (i + 1) * BLOCK]
        start = i * BLOCK
        first = min(width, rot_ref.shape[1] - start)
        spans = [(0, start, first)]
        if first < width:
            spans.append((first, 0, width - first))
        for at, col, wide in spans:
            out_ref[i * BLOCK : (i + 1) * BLOCK, at : at + wide] = lax.dot_general(
                left,
                app_ref[:, col : col + wide],
                (((0,), (0,)), ((), ())),
                preferred_element_type=jnp.float32,
            ).astype(out_ref.dtype)


def spread(packed_ref, full, first, last):
    blocks = full.shape[0] // BLOCK
    half = packed_ref.shape[1] // BLOCK - 1
    for i in range(first, last):
        for k in range(half + 1):
            j = (i + k) % blocks
            tile = packed_ref[i * BLOCK : (i + 1) * BLOCK, k * BLOCK : (k + 1) * BLOCK]
            full[i * BLOCK : (i + 1) * BLOCK, j * BLOCK : (j + 1) * BLOCK] = tile
            if 0 < k < half:
                full[j * BLOCK : (j + 1) * BLOCK, i * BLOCK : (i + 1) * BLOCK] = tile.T


def horner(coeffs, orb_ref, rot_ref, full, columns, emit):
    cos_coeffs, sin_coeffs = coeffs
    orb = orb_ref[...].astype(jnp.float32)
    rot = rot_ref[...].astype(jnp.float32)
    current = (cos_coeffs[ORDER] * orb + sin_coeffs[ORDER] * rot).astype(jnp.bfloat16)
    for degree in range(ORDER - 1, -1, -1):
        parts = []
        for c in range(0, orb_ref.shape[1], columns):
            total = jnp.dot(current, full[:, c : c + columns], preferred_element_type=jnp.float32)
            o = orb_ref[:, c : c + columns].astype(jnp.float32)
            r = rot_ref[:, c : c + columns].astype(jnp.float32)
            part = (total + cos_coeffs[degree] * o + sin_coeffs[degree] * r).astype(jnp.bfloat16)
            if degree == 0:
                emit(c, part)
            parts.append(part)
        if degree:
            current = jnp.concatenate(parts, axis=1)


def exchange_kernel(
    tracks, scale, coeffs, packed_ref, orb_ref, rot_ref, wide_ref, rotated_ref, fock_ref,
    got, acc, send, out_ref, full, ext, send_sem, recv_sem, halo_send, halo_recv,
):
    size = lax.axis_size("row")
    me = lax.axis_index("row")
    steps = size.bit_length() - 1
    width = packed_ref.shape[1]
    rows = packed_ref.shape[0] // tracks
    half = rows // 2
    outer = [1 << b for b in range(1, steps)]
    swapped = [outer[1], outer[0]] + outer[2:] if len(outer) > 1 else outer
    third = outer[2:3] + outer[:2] + outer[3:]
    orders = [[1] + (outer, swapped, third)[t % 3] for t in range(tracks)]

    def high(bit):
        return lax.rem(me // bit, 2)

    def partner(bit):
        return me + bit - 2 * bit * high(bit)

    def span(start, count):
        return pl.ds(pl.multiple_of(start, 16), count)

    def copy(source, target, t, step, bit):
        return pltpu.make_async_remote_copy(
            src_ref=source,
            dst_ref=target,
            send_sem=send_sem.at[t, step],
            recv_sem=recv_sem.at[t, step],
            device_id={"row": partner(bit)},
            device_id_type=pl.DeviceIdType.MESH,
        )

    barrier = pltpu.get_barrier_semaphore()
    for b in range(steps):
        pl.semaphore_signal(
            barrier, inc=1, device_id={"row": partner(1 << b)}, device_id_type=pl.DeviceIdType.MESH
        )
    below, above = me > 0, me < size - 1
    inner = jnp.logical_and(below, above)

    @pl.when(inner)
    def _():
        pl.semaphore_signal(
            barrier,
            inc=1,
            device_id={"row": me - 1 + 2 * lax.rem(me, 2)},
            device_id_type=pl.DeviceIdType.MESH,
        )
        pl.semaphore_wait(barrier, steps + 1)

    @pl.when(jnp.logical_not(inner))
    def _():
        pl.semaphore_wait(barrier, steps)

    local, wing = orb_ref.shape[0], 2 * BLOCK

    @pl.when(me == 0)
    def _():
        ext[:wing, :] = jnp.zeros((wing, ext.shape[1]), ext.dtype)

    @pl.when(me == size - 1)
    def _():
        ext[local + wing :, :] = jnp.zeros((wing, ext.shape[1]), ext.dtype)

    copies = []
    pending = []
    offsets = [0] * tracks
    for t in range(tracks):
        c = copy(
            packed_ref.at[span(t * rows + (1 - high(1)) * half, half)],
            got.at[pl.ds(t * rows, half)],
            t, 0, 1,
        )
        c.start()
        copies.append(c)
        pending.append(c)

    for step in range(steps):
        count = rows >> (step + 1)
        landed = rows - (rows >> step)
        for t in range(tracks):
            pending[t].wait_recv()
            base = offsets[t]

            def total(shift, number):
                more = got[span(t * rows + landed + shift, number), :].astype(jnp.float32)
                if step == 0:
                    own = packed_ref[span(t * rows + high(1) * half + shift, number), :]
                    return own.astype(jnp.float32) + more
                return acc[span(t * half + base + shift, number), :] + more

            if step < steps - 1:
                bit = orders[t][step + 1]
                part = count // 2
                away, kept = (1 - high(bit)) * part, high(bit) * part
                place = span(t * half + base + away, part)
                send[place, :] = total(away, part).astype(send.dtype)
                c = copy(
                    send.at[place],
                    got.at[pl.ds(t * rows + landed + count, part)],
                    t, step + 1, bit,
                )
                c.start()
                acc[span(t * half + base + kept, part), :] = total(kept, part)
                offsets[t] = base + kept
            else:
                offsets[t] = t * rows + high(1) * half + base
                place = span(offsets[t], count)
                out_ref[place, :] = (total(0, count) * scale).astype(out_ref.dtype)
                c = copy(out_ref.at[place], out_ref.at[place], t, steps, orders[t][step])
                c.start()
            copies.append(c)
            pending[t] = c

    count = rows >> steps
    for step in range(steps):
        for t in range(tracks):
            bit = orders[t][steps - 1 - step]
            pending[t].wait_recv()
            offsets[t] = offsets[t] - high(bit) * count
            if step < steps - 1:
                place = span(offsets[t], 2 * count)
                c = copy(
                    out_ref.at[place], out_ref.at[place], t, steps + step + 1,
                    orders[t][steps - 2 - step],
                )
                c.start()
                copies.append(c)
                pending[t] = c
            else:
                spread(out_ref, full, t * rows // BLOCK, (t + 1) * rows // BLOCK)
        count = 2 * count

    columns = CHUNK

    def halo_copy(side, c):
        source, target, index = ((wing, local + wing, me - 1), (local, 0, me + 1))[side]
        return pltpu.make_async_remote_copy(
            src_ref=ext.at[pl.ds(source, wing), pl.ds(c, columns)],
            dst_ref=ext.at[pl.ds(target, wing), pl.ds(c, columns)],
            send_sem=halo_send.at[side, c // columns],
            recv_sem=halo_recv.at[side, c // columns],
            device_id={"row": index},
            device_id_type=pl.DeviceIdType.MESH,
        )

    def emit(c, part):
        rotated_ref[:, c : c + columns] = part
        ext[wing : wing + local, c : c + columns] = part
        for side, there in ((0, below), (1, above)):

            @pl.when(there)
            def _():
                halo_copy(side, c).start()

    horner(coeffs, orb_ref, rot_ref, full, columns, emit)
    for c in range(0, orb_ref.shape[1], columns):
        for side, there in ((0, above), (1, below)):

            @pl.when(there)
            def _():
                halo_copy(side, c).wait_recv()

        for at in range(0, local, BLOCK):
            fock_ref[at : at + BLOCK, c : c + columns] = jnp.dot(
                wide_ref[at : at + BLOCK, :],
                ext[at : at + 5 * BLOCK, c : c + columns],
                preferred_element_type=jnp.float32,
            )
    for c in range(0, orb_ref.shape[1], columns):
        for side, there in ((0, below), (1, above)):

            @pl.when(there)
            def _():
                halo_copy(side, c).wait_send()

    for c in copies:
        c.wait_send()


def exchange(packed, orbitals, rotation, wide, scale, coeffs):
    size = lax.axis_size("row")
    rows, width = packed.shape
    steps = size.bit_length() - 1
    tracks = max(1, min(TRACKS, rows // (16 * size)))
    return pl.pallas_call(
        functools.partial(exchange_kernel, tracks, scale, coeffs),
        out_shape=(
            jax.ShapeDtypeStruct(orbitals.shape, jnp.bfloat16),
            jax.ShapeDtypeStruct(orbitals.shape, jnp.float32),
        ),
        in_specs=[pl.BlockSpec(memory_space=pltpu.VMEM)] * 4,
        out_specs=(pl.BlockSpec(memory_space=pltpu.VMEM),) * 2,
        scratch_shapes=[
            pltpu.VMEM((rows, width), SENT),
            pltpu.VMEM((rows // 2, width), jnp.float32),
            pltpu.VMEM((rows // 2, width), SENT),
            pltpu.VMEM((rows, width), jnp.bfloat16),
            pltpu.VMEM((rows, rows), jnp.bfloat16),
            pltpu.VMEM((orbitals.shape[0] + 4 * BLOCK, rows), jnp.bfloat16),
            pltpu.SemaphoreType.DMA((tracks, 2 * steps)),
            pltpu.SemaphoreType.DMA((tracks, 2 * steps)),
            pltpu.SemaphoreType.DMA((2, rows // CHUNK)),
            pltpu.SemaphoreType.DMA((2, rows // CHUNK)),
        ],
        compiler_params=pltpu.CompilerParams(
            collective_id=0, has_side_effects=True, vmem_limit_bytes=56 * 2**20
        ),
    )(packed, orbitals, rotation, wide)


def shards(orbitals, rotation, fock_tiles, fock_pattern, correlation_tiles, correlation_pattern):
    tile_size = correlation_tiles.shape[2]
    local_rows, orbital_count = rotation.shape
    size = lax.axis_size("row")
    basis_total = local_rows * size
    half = orbital_count // BLOCK // 2
    width = (half + 1) * BLOCK
    cos_coeffs = [(-1.0) ** degree / math.factorial(2 * degree) for degree in range(ORDER + 1)]
    sin_coeffs = [(-1.0) ** degree / math.factorial(2 * degree + 1) for degree in range(ORDER + 1)]
    extended = halo(rotation, 2 * tile_size)
    applied = near_product(wide_tiles(correlation_tiles, correlation_pattern), extended)
    applied = applied.astype(jnp.bfloat16)
    packed = pl.pallas_call(
        functools.partial(gram_kernel, half),
        out_shape=jax.ShapeDtypeStruct((orbital_count, width), SENT),
        in_specs=[pl.BlockSpec(memory_space=pltpu.VMEM)] * 2,
        out_specs=pl.BlockSpec(memory_space=pltpu.VMEM),
        compiler_params=pltpu.CompilerParams(vmem_limit_bytes=40 * 2**20),
    )(rotation, applied)

    wide = wide_tiles(fock_tiles, fock_pattern)
    return exchange(
        packed, orbitals, rotation, wide, 4.0 / basis_total, (cos_coeffs, sin_coeffs)
    )


def solution(mesh):
    rows = P(("group", "row"), None)
    tiles = P(("group", "row"), None, None, None)
    return jax.shard_map(
        shards,
        mesh=mesh,
        in_specs=(rows, rows, tiles, rows, tiles, rows),
        out_specs=(rows, rows),
        check_vma=False,
    )
```
